128 devices in a mesh: tm: 8 (over x, y_hi), space: 16 (over y_lo, z, core).
Axes of the slice: x: 4, y: 4 (y_hi: 2, y_lo: 2; y = y_hi * 2 + y_lo), z: 4, core: 2. Of those that a mesh axis runs over, the one named last changes fastest.
Arguments:
- video: bfloat16 [32, 32, 24, 3072], P('tm', 'space'), may hold values from -6 to 6
- w_qkv: bfloat16 [3072, 16, 384], P(None, 'space'), may hold values from -0.109375 to 0.109375
- w_out: bfloat16 [16, 128, 3072], P('space'), may hold values from -0.5 to 0.5
- q_gain: float32 [128], replicated, may hold values from 1 to 8
- k_gain: float32 [128], replicated, may hold values from 1 to 8
- tile_perm: int32 [8, 3072], P('tm'), may hold values from 0 to 3071, as said below
- window: int32 [12, 6], replicated, may hold values from 0 to 11, as said below
Outputs:
- mixed: bfloat16 [8, 3072, 3072], P('tm', 'space')
The draws below stay inside these ranges and needn't reach their ends.
Inputs may be any that keep to these rules, and one draw needn't show every extreme that they name: `tile_perm`: each row is a permutation of the slots of one frame group in which slots t*256 to t*256 + 255 hold exactly the tokens of tile t; tile t covers frames of the group, rows (t // 3) * 8 onward and columns (t % 3) * 8 onward, 8 and 8 of them. `window`: row t holds 6 different tiles, the first being t.
All inputs are finite; a program needn't handle non-finite values.
Results may differ from the reference program's by a relative error of at most 0.023.
The reference program's roundings to bfloat16 on the way count: a program that leaves them out, or rounds other values in their place, can miss the bound.
Values may be sent and summed in bfloat16 or wider, within the bound.
No kernel may reach another device: no remote copies, remote signals or barrier semaphores. Data moves between devices by JAX's collectives and lax.ppermute only.
A program may use at most 128 MiB of HBM per device.

```python
import jax
import jax.numpy as jnp
from jax import lax

D = 3072
HD = 128
HEAD_DEV = 1
HEADS = 16
TH = 8
TW = 8
WIN = 6
W = 24
ROWS = 32
GROUPS = 8
FRAMES = 32
TILE = 256
NTS = 12
GTOK = 3072
N_SPACE = 16


def gain_values(key):
    return jnp.exp(jax.random.uniform(key, (HD,), jnp.float32, 0.0, 1.0986))


def draw_q_gain(key, part):
    key = jax.random.fold_in(key, 13)
    return gain_values(key)


def draw_k_gain(key, part):
    key = jax.random.fold_in(key, 14)
    return gain_values(key)


def draw_tile_perm(key, part):
    key = jax.random.fold_in(key, 11)
    tile_cols = W // TW
    slot = jnp.arange(GTOK, dtype=jnp.int32)
    tile_index = slot // TILE
    inner = slot % TILE
    tile_row = tile_index // tile_cols
    tile_col = tile_index % tile_cols
    frame = inner // (TH * TW)
    row_in = inner // TW % TH
    col_in = inner % TW
    raster = frame * ROWS * W + (tile_row * TH + row_in) * W + tile_col * TW + col_in
    base = raster.reshape(NTS, TILE)
    scores = jax.random.randint(key, (GROUPS, NTS, TILE), 0, 1 << 20, jnp.int32) * TILE
    scores = scores + jnp.arange(TILE, dtype=jnp.int32)[None, None, :]
    order = jnp.argsort(scores, axis=-1).astype(jnp.int32)
    shuffled = jnp.take_along_axis(jnp.broadcast_to(base[None], (GROUPS, NTS, TILE)), order, axis=-1)
    return shuffled.reshape(GROUPS, GTOK).astype(jnp.int32)


def draw_window(key, part):
    key = jax.random.fold_in(key, 12)
    scores = jax.random.randint(key, (NTS, NTS), 0, 1 << 20, jnp.int32) * NTS
    scores = scores + jnp.arange(NTS, dtype=jnp.int32)[None, :]
    scores = jnp.where(jnp.eye(NTS, dtype=jnp.bool_), -1, scores)
    return jnp.argsort(scores, axis=1)[:, :WIN].astype(jnp.int32)


def block_scale(own_key, extent, shards, least, top_value):
    def one(axis_at, blocks):
        steps = jax.random.uniform(jax.random.fold_in(jax.random.fold_in(own_key, 6), axis_at), (blocks,), jnp.float32, least / len(shards), top_value / len(shards))
        return jnp.repeat(jnp.exp(steps), extent[axis_at] // blocks).reshape((-1,) + (1,) * (len(extent) - axis_at - 1))

    loudness = one(*shards[0])
    for cut in shards[1:]:
        loudness = loudness * one(*cut)
    return loudness


def normal_values(key, extent, scale, most, pieces=(), kind=jnp.bfloat16):
    factor_of = block_scale(key, extent, pieces, -0.22, 0.18) if pieces else 1.0
    values = jax.random.normal(key, extent, jnp.float32) * scale * factor_of
    return jnp.minimum(jnp.maximum(values, -most), most).astype(kind)


def setup_inputs(seed: int = 0) -> dict:
    streams_of = jax.random.split(jax.random.key(seed), 8)
    video = normal_values(streams_of[0], (FRAMES, ROWS, W, D), 1.0, 6.0, ((0, 8), (1, 16)))
    w_qkv = normal_values(streams_of[1], (D, HEADS, 3 * HD), D ** -0.5, 0.109375, ((1, 16),))
    w_out = normal_values(streams_of[2], (HEADS, HD, D), HD ** -0.5, 0.5, ((0, 16),))
    q_gain = draw_q_gain(jax.random.fold_in(streams_of[7], 71), 0)
    k_gain = draw_k_gain(jax.random.fold_in(streams_of[7], 71), 0)
    tile_perm = draw_tile_perm(jax.random.fold_in(streams_of[7], 71), 0)
    window = draw_window(jax.random.fold_in(streams_of[7], 71), 0)
    return dict(video=video, w_qkv=w_qkv, w_out=w_out, q_gain=q_gain, k_gain=k_gain, tile_perm=tile_perm, window=window)


def head_norm(values, gain):
    wide = values.astype(jnp.float32)
    scaled = wide * lax.rsqrt(lax.optimization_barrier(jnp.mean(wide * wide, axis=-1, keepdims=True)) + 1e-06)
    return (scaled * gain).astype(jnp.bfloat16)

def attend(queries, chosen, valid):
    heads_here = queries.shape[1]
    head_dim = queries.shape[2]
    span = chosen.shape[1] * chosen.shape[2]
    keys = chosen[:, :, :, :, 0, :].reshape(-1, heads_here, head_dim)
    values = chosen[:, :, :, :, 1, :].reshape(-1, heads_here, head_dim)
    scores = jnp.einsum('qhd,khd->hqk', queries.astype(jnp.float32), keys.astype(jnp.float32)) * head_dim ** (-0.5)
    live = jnp.repeat(valid, span)
    scores = jnp.where(live[None, None, :], scores, -jnp.inf)
    highest = lax.optimization_barrier(jnp.max(scores, axis=-1, keepdims=True))
    weights = jnp.exp(scores - highest)
    probs = (weights / lax.optimization_barrier(jnp.sum(weights, axis=-1, keepdims=True))).astype(jnp.bfloat16)
    result = jnp.einsum('hqk,khd->qhd', probs.astype(jnp.float32), values.astype(jnp.float32))
    return result.astype(jnp.bfloat16)

def reference(video, w_qkv, w_out, q_gain, k_gain, tile_perm, window):
    flat_w = w_qkv.reshape(D, HEADS * 3 * HD)
    tokens = video.reshape(GROUPS, GTOK, D)

    def project(pair):
        group_tokens, order = pair
        qkv = jnp.dot(group_tokens, flat_w, preferred_element_type=jnp.float32).astype(jnp.bfloat16)
        qkv = qkv.reshape(GTOK, HEADS, 3, HD)
        ordered = jnp.take(qkv, order, axis=0)
        queries = head_norm(ordered[:, :, 0, :], q_gain)
        keys = head_norm(ordered[:, :, 1, :], k_gain)
        return (queries, jnp.stack([keys, ordered[:, :, 2, :]], axis=2))
    query_all, pairs_all = lax.map(project, (tokens, tile_perm))
    pairs_all = pairs_all.reshape(GROUPS, NTS, TILE, HEADS, 2, HD)
    blank = jnp.zeros((1,) + pairs_all.shape[1:], jnp.bfloat16)
    padded = jnp.concatenate([blank, pairs_all, blank], axis=0)

    def group_out(group_index):
        near = lax.dynamic_slice_in_dim(padded, group_index, 3, 0)
        valid = jnp.stack([group_index > 0, group_index >= 0, group_index < GROUPS - 1])
        query_group = lax.dynamic_index_in_dim(query_all, group_index, 0, keepdims=False)
        query_tiles = query_group.reshape(NTS, TILE, HEADS, HD)

        def one_tile(item):
            block, picks = item
            return attend(block, jnp.take(near, picks, axis=1), valid)
        return lax.map(one_tile, (query_tiles, window)).reshape(GTOK, HEADS * HD)
    attn_all = lax.map(group_out, jnp.arange(GROUPS, dtype=jnp.int32))
    flat_attn = attn_all.reshape(GROUPS * GTOK, N_SPACE, HEAD_DEV * HD)
    out_w = w_out.reshape(N_SPACE, HEAD_DEV * HD, D)

    def add_group(total, index):
        part_in = lax.dynamic_index_in_dim(flat_attn, index, 1, keepdims=False)
        part_w = lax.dynamic_index_in_dim(out_w, index, 0, keepdims=False)
        term = jnp.dot(part_in, part_w, preferred_element_type=jnp.float32)
        rounded = lax.optimization_barrier(term.astype(jnp.bfloat16)).astype(jnp.float32)
        return (total + rounded, None)
    start_total = jnp.zeros((GROUPS * GTOK, D), jnp.float32)
    total, unused = lax.scan(add_group, start_total, jnp.arange(N_SPACE, dtype=jnp.int32))
    return total.astype(jnp.bfloat16).reshape(GROUPS, GTOK, D)
```

```python
import jax
import jax.numpy as jnp
from jax import lax
from jax.experimental import pallas as pl
from jax.experimental.pallas import tpu as pltpu
from jax.sharding import Mesh
from jax.sharding import PartitionSpec as P

D = 3072
HD = 128
NT = 12
TILE = 256
WIN = 6
AXES = ("x", "yh", "yl", "z", "c")
SIZES = (4, 2, 2, 4, 2)
VMEM = 56 * 1024 * 1024


def move(value, target):
    pairs = []
    for x in range(4):
        for y in range(4):
            for z in range(4):
                for c in range(2):
                    goal = target(x, y, z, c)
                    if goal is None:
                        continue
                    a, b, d, e = goal
                    pairs.append(
                        (((x * 4 + y) * 4 + z) * 2 + c, ((a * 4 + b % 4) * 4 + d) * 2 + e)
                    )
    return lax.ppermute(value, AXES, pairs)


def across(k):
    return lambda x, y, z, c: (x, y, z ^ k, c)


def swap_core(x, y, z, c):
    return (x, y, z, 1 - c)


def up(x, y, z, c):
    return (x, y + 1, z, c)


def down(x, y, z, c):
    return (x, y - 1, z, c)


def regroup(k):
    return lambda x, y, z, c: (x, 2 * c + ((y & 1) ^ k), z, y >> 1)


def beside(x, y, z, c):
    if c == 1:
        return (x + 1, y, z, 0) if x < 3 else None
    return (x - 1, y, z, 1) if x > 0 else None


def normed(part, gain):
    wide = part.astype(jnp.float32)
    mean = jnp.mean(wide * wide, axis=-1, keepdims=True)
    return (wide * lax.rsqrt(mean + 1e-06) * gain).astype(jnp.bfloat16)


def project_body(rows, places, aliased, *refs):
    count = len(rows)
    xs = refs[:count]
    own_w, low_w, high_w, gain_q, gain_k = refs[count : count + 5]
    refs = refs[count + 5 + (4 if aliased else 0) :]
    outs = refs[:4]
    x_buf, w_buf, stage, x_sem, w_sem, out_sem = refs[4:]
    half = D // 2
    w_copies = [
        pltpu.make_async_copy(own_w, w_buf.at[:, 0:384], w_sem.at[0]),
        pltpu.make_async_copy(low_w, w_buf.at[0:half, 384:768], w_sem.at[1]),
        pltpu.make_async_copy(high_w, w_buf.at[half:D, 384:768], w_sem.at[2]),
    ]
    for copy in w_copies:
        copy.start()
    x_copies = []
    for i in range(count):
        copy = pltpu.make_async_copy(xs[i], x_buf.at[i, 0 : rows[i]], x_sem.at[i])
        copy.start()
        x_copies.append(copy)
    for copy in w_copies:
        copy.wait()
    out_copies = []
    for i in range(count):
        x_copies[i].wait()
        n = rows[i]
        lines = n // 24
        y = jnp.dot(x_buf[i, 0:n], w_buf[...], preferred_element_type=jnp.float32)
        y = y.astype(jnp.bfloat16)
        for h in range(2):
            q = normed(y[:, h * 384 : h * 384 + 128], gain_q[...])
            k = normed(y[:, h * 384 + 128 : h * 384 + 256], gain_k[...])
            v = y[:, h * 384 + 256 : h * 384 + 384]
            for value, base in ((q, 0), (k, 128), (v, 256)):
                tall = value.astype(jnp.float32).reshape(lines, 3, 8, 128)
                for tc in range(3):
                    stage[i, h, tc, 0 : lines * 8, base : base + 128] = (
                        tall[:, tc].reshape(lines * 8, 128).astype(jnp.bfloat16)
                    )
        row, blk, off = places[i]
        for h in range(2):
            for tc in range(3):
                for j, (lo, hi) in enumerate(((0, 128), (128, 384))):
                    copy = pltpu.make_async_copy(
                        stage.at[i, h, tc, 0 : lines * 8, lo:hi],
                        outs[2 * h + j].at[row, tc, blk, off : off + lines * 8],
                        out_sem.at[i],
                    )
                    copy.start()
                    out_copies.append(copy)
    for copy in out_copies:
        copy.wait()


def project(xs, places, own_w, low_w, high_w, gain_q, gain_k, previous=None):
    rows = [x.shape[0] for x in xs]
    count = len(xs)
    any_spec = pl.BlockSpec(memory_space=pl.ANY)
    vmem_spec = pl.BlockSpec(memory_space=pltpu.VMEM)
    shapes = []
    for _ in range(2):
        shapes.append(jax.ShapeDtypeStruct((2, 3, 4, 64, 128), jnp.bfloat16))
        shapes.append(jax.ShapeDtypeStruct((2, 3, 4, 64, 256), jnp.bfloat16))
    extra = [] if previous is None else list(previous)

    def body(*refs):
        project_body(rows, places, previous is not None, *refs)

    return pl.pallas_call(
        body,
        out_shape=shapes,
        in_specs=[any_spec] * (count + 3) + [vmem_spec] * 2 + [any_spec] * len(extra),
        out_specs=[any_spec] * 4,
        scratch_shapes=[
            pltpu.VMEM((count, max(rows), D), jnp.bfloat16),
            pltpu.VMEM((D, 768), jnp.bfloat16),
            pltpu.VMEM((count, 2, 3, 64, 384), jnp.bfloat16),
            pltpu.SemaphoreType.DMA((count,)),
            pltpu.SemaphoreType.DMA((3,)),
            pltpu.SemaphoreType.DMA((count,)),
        ],
        input_output_aliases={count + 5 + i: i for i in range(len(extra))},
        compiler_params=pltpu.CompilerParams(vmem_limit_bytes=VMEM),
        cost_estimate=pl.CostEstimate(
            flops=2 * sum(rows) * D * 768,
            bytes_accessed=sum(rows) * D * 2 + D * 768 * 2,
            transcendentals=0,
        ),
        name="project",
    )(*xs, own_w, low_w, high_w, gain_q, gain_k, *extra)


def attend_body(
    picks, facts, q0, q1, k00, k01, k10, k11, k20, k21, inner, out, q_buf, kv, scores, sem
):
    copies = []
    for i, (src, dst) in enumerate(
        (
            (q0, q_buf.at[0:6]),
            (q1, q_buf.at[6:12]),
            (k00, kv.at[0, 0:6]),
            (k01, kv.at[0, 6:12]),
            (k10, kv.at[1, 0:6]),
            (k11, kv.at[1, 6:12]),
            (k20, kv.at[2, 0:6]),
            (k21, kv.at[2, 6:12]),
        )
    ):
        copy = pltpu.make_async_copy(src, dst, sem.at[i])
        copy.start()
        copies.append(copy)
    for copy in copies:
        copy.wait()
    rel_row, rel_half, core, valid = facts[0], facts[1], facts[2], facts[3]
    scale = HD**-0.5 * 1.4426950408889634
    shift = jnp.where(valid > 0, 0.0, 1e30).astype(jnp.float32)

    def place(t):
        half = t // 6
        row = (t // 3) % 2
        return (half ^ rel_half) * 6 + (row ^ rel_row) * 3 + t % 3

    @pl.loop(0, NT)
    def _(t):
        q = q_buf[place(t)]
        where = [place(picks[t, j]) for j in range(WIN)]
        tops = []
        for g in range(3):
            top = None
            for j in range(WIN):
                s = lax.dot_general(
                    q,
                    kv[g, where[j], :, 0:HD],
                    (((1,), (1,)), ((), ())),
                    preferred_element_type=jnp.float32,
                )
                scores[g * WIN + j] = s
                high = jnp.maximum(s[:, 0:128], s[:, 128:256])
                top = high if top is None else jnp.maximum(top, high)
            tops.append(jnp.max(top, axis=-1, keepdims=True))
        tops[2] = tops[2] - shift
        m = jnp.maximum(jnp.maximum(tops[0], tops[1]), tops[2]) * scale
        m_far = m + shift
        total = jnp.zeros((TILE, 128), jnp.float32)
        acc = jnp.zeros((TILE, HD), jnp.float32)
        for g in range(3):
            base = m_far if g == 2 else m
            for j in range(WIN):
                p = jnp.exp2(scores[g * WIN + j] * scale - base)
                total = total + (p[:, 0:128] + p[:, 128:256])
                acc = acc + jnp.dot(
                    p.astype(jnp.bfloat16),
                    kv[g, where[j], :, HD : 2 * HD],
                    preferred_element_type=jnp.float32,
                )
        attn = (acc / jnp.sum(total, axis=-1, keepdims=True)).astype(jnp.bfloat16)
        columns = lax.broadcasted_iota(jnp.int32, (TILE, TILE), 1)
        pick = (inner[t] == columns).astype(jnp.float32).astype(jnp.bfloat16)
        ordered = jnp.dot(pick, attn, preferred_element_type=jnp.float32).astype(jnp.bfloat16)
        for i in range(4):
            piece = 4 * t + i
            owner = piece // 3
            out[(owner % 2) ^ core, owner // 2, piece % 3] = ordered[i * 64 : i * 64 + 64]


def attend(picks, facts, qs, kvs, inner):
    any_spec = pl.BlockSpec(memory_space=pl.ANY)
    vmem_spec = pl.BlockSpec(memory_space=pltpu.VMEM)
    smem_spec = pl.BlockSpec(memory_space=pltpu.SMEM)
    keys = 3 * WIN * TILE
    return pl.pallas_call(
        attend_body,
        out_shape=jax.ShapeDtypeStruct((2, 8, 3, 64, HD), jnp.bfloat16),
        in_specs=[smem_spec] * 2 + [any_spec] * 8 + [vmem_spec],
        out_specs=vmem_spec,
        scratch_shapes=[
            pltpu.VMEM((NT, TILE, HD), jnp.bfloat16),
            pltpu.VMEM((3, NT, TILE, 2 * HD), jnp.bfloat16),
            pltpu.VMEM((3 * WIN, TILE, TILE), jnp.float32),
            pltpu.SemaphoreType.DMA((8,)),
        ],
        compiler_params=pltpu.CompilerParams(vmem_limit_bytes=VMEM),
        cost_estimate=pl.CostEstimate(
            flops=4 * NT * TILE * keys * HD,
            bytes_accessed=6_000_000,
            transcendentals=NT * TILE * keys,
        ),
        name="attend",
    )(picks, facts, *qs, *kvs, inner)


def mix_body(attn, w, out):
    parts = [None] * 16
    for yh in range(2):
        for yl in range(2):
            for z in range(4):
                parts[yl * 8 + z * 2 + yh] = attn[(yh * 2 + yl) * 4 + z]
    flat = jnp.concatenate(parts, axis=-1)
    out[...] = jnp.dot(flat, w[...], preferred_element_type=jnp.float32).astype(jnp.bfloat16)


def mix(attn, w):
    step = 512
    return pl.pallas_call(
        mix_body,
        out_shape=jax.ShapeDtypeStruct((192, D), jnp.bfloat16),
        grid=(D // step,),
        in_specs=[
            pl.BlockSpec((16, 192, HD), lambda i: (0, 0, 0)),
            pl.BlockSpec((16 * HD, step), lambda i: (0, i)),
        ],
        out_specs=pl.BlockSpec((192, step), lambda i: (0, i)),
        compiler_params=pltpu.CompilerParams(vmem_limit_bytes=VMEM),
        cost_estimate=pl.CostEstimate(
            flops=2 * 192 * 2048 * D, bytes_accessed=14_000_000, transcendentals=0
        ),
        name="mix",
    )(attn, w)


def per_device(video, w_qkv, w_out, q_gain, k_gain, tile_perm, window):
    x_at, yh, yl, z, c = (lax.axis_index(a) for a in AXES)
    own = video.reshape(192, D)
    own_w = w_qkv.reshape(D, 384)
    gain_q = q_gain.reshape(1, HD)
    gain_k = k_gain.reshape(1, HD)

    near = move(own, across(1))
    rear = move(own, across(3))
    low_w = move(own_w[: D // 2], up)
    high_w = move(own_w[D // 2 :], down)
    own_other = move(own, swap_core)
    half = 96
    far_a = move(rear[:half], across(1))
    far_b = move(near[half:], across(3))
    near_other = move(near, swap_core)
    rear_other = move(rear, swap_core)
    far_a_other = move(far_a, swap_core)
    far_b_other = move(far_b, swap_core)

    first = project(
        [own, own_other, near, near_other, rear, rear_other],
        [(0, 0, 0), (0, 1, 0), (0, 2, 0), (0, 3, 0), (1, 2, 0), (1, 3, 0)],
        own_w, low_w, high_w, gain_q, gain_k,
    )
    q_a, kv_a, q_b, kv_b = project(
        [far_a, far_b, far_a_other, far_b_other],
        [(1, 0, 0), (1, 0, 32), (1, 1, 0), (1, 1, 32)],
        own_w, low_w, high_w, gain_q, gain_k, first,
    )
    kv0 = move(kv_a, regroup(0))
    kv1 = move(kv_b, regroup(1))
    q0 = move(q_a, regroup(0))
    q1 = move(q_b, regroup(1))
    kvs = [kv0, kv1, move(kv0, swap_core), move(kv1, swap_core), move(kv0, beside), move(kv1, beside)]

    raster = move(tile_perm.reshape(NT, TILE), regroup(0))
    frame, rest = raster // 768, raster % 768
    line, column = (rest // 24) % 8, rest % 8
    block = ((line // 4) ^ (z % 2)) * 2 + (((line // 2) % 2) ^ yh)
    inner = block * 64 + frame * 16 + (line % 2) * 8 + column
    valid = jnp.where(c == 0, x_at > 0, x_at < 3).astype(jnp.int32)
    facts = jnp.stack([z // 2, yl, c, valid]).astype(jnp.int32)
    attn = attend(
        window,
        facts,
        [q.reshape(6, TILE, HD) for q in (q0, q1)],
        [k.reshape(6, TILE, 2 * HD) for k in kvs],
        inner.reshape(NT, TILE, 1),
    )
    other = move(attn[1], swap_core)
    both = jnp.where(c == 0, jnp.stack([attn[0], other]), jnp.stack([other, attn[0]]))
    spread = lax.all_to_all(
        both.reshape(16, 192, HD), ("yh", "yl", "z"), 0, 0, tiled=True
    )
    w_all = lax.all_gather(w_out, ("yl", "z", "c"), axis=0, tiled=True)
    return mix(spread, w_all.reshape(16 * HD, D))[None]


def solution(mesh):
    fine = Mesh(mesh.devices.reshape(SIZES), AXES)
    tm = ("x", "yh")
    space = ("yl", "z", "c")
    in_specs = (
        P(tm, space, None, None),
        P(None, space, None),
        P(space, None, None),
        P(),
        P(),
        P(tm, None),
        P(),
    )
    return jax.shard_map(
        per_device, mesh=fine, in_specs=in_specs, out_specs=P(tm, space, None), check_vma=False
    )
```

```python
import jax
import jax.numpy as jnp
from jax import lax
from jax.experimental import pallas as pl
from jax.experimental.pallas import tpu as pltpu
from jax.sharding import Mesh
from jax.sharding import PartitionSpec as P

D = 3072
HD = 128
NT = 12
TILE = 256
WIN = 6
AXES = ("x", "yh", "yl", "z", "c")
SIZES = (4, 2, 2, 4, 2)
VMEM = 60 * 1024 * 1024


def move(value, target):
    pairs = []
    for x in range(4):
        for y in range(4):
            for z in range(4):
                for c in range(2):
                    goal = target(x, y, z, c)
                    if goal is None:
                        continue
                    a, b, d, e = goal
                    pairs.append(
                        (((x * 4 + y) * 4 + z) * 2 + c, ((a * 4 + b % 4) * 4 + d) * 2 + e)
                    )
    return lax.ppermute(value, AXES, pairs)


def after(value, *others):
    return lax.optimization_barrier((value,) + others)[0]


def across(k):
    return lambda x, y, z, c: (x, y, z ^ k, c)


def swap_core(x, y, z, c):
    return (x, y, z, 1 - c)


def up(x, y, z, c):
    return (x, y + 1, z, c)


def down(x, y, z, c):
    return (x, y - 1, z, c)


def regroup(k):
    return lambda x, y, z, c: (x, 2 * c + ((y & 1) ^ k), z, y >> 1)


def beside(x, y, z, c):
    if c == 1:
        return (x + 1, y, z, 0) if x < 3 else None
    return (x - 1, y, z, 1) if x > 0 else None


def normed(part, gain):
    wide = part.astype(jnp.float32)
    mean = jnp.mean(wide * wide, axis=-1, keepdims=True)
    return (wide * lax.rsqrt(mean + 1e-06) * gain).astype(jnp.bfloat16)


def project_body(rows, places, *refs):
    count = len(rows)
    xs = refs[:count]
    own_w, low_w, high_w, gain_q, gain_k, out0, out1 = refs[count : count + 7]
    outs = (out0, out1)
    x_buf, w_buf, stage, x_sem, w_sem, out_sem = refs[count + 7 :]
    half = D // 2
    starts = [sum(rows[:i]) for i in range(count)]
    w_copies = [
        pltpu.make_async_copy(own_w, w_buf.at[:, 0:384], w_sem.at[0]),
        pltpu.make_async_copy(low_w, w_buf.at[0:half, 384:768], w_sem.at[1]),
        pltpu.make_async_copy(high_w, w_buf.at[half:D, 384:768], w_sem.at[2]),
    ]
    for copy in w_copies:
        copy.start()
    x_copies = []
    for i in range(count):
        copy = pltpu.make_async_copy(
            xs[i], x_buf.at[starts[i] : starts[i] + rows[i]], x_sem.at[i]
        )
        copy.start()
        x_copies.append(copy)
    for copy in w_copies:
        copy.wait()
    out_copies = []
    at = 0
    while at < count:
        members = [at]
        while sum(rows[i] for i in members) < 384:
            members.append(members[-1] + 1)
        at = members[-1] + 1
        for i in members:
            x_copies[i].wait()
        base, n = starts[members[0]], 384
        y = jnp.dot(x_buf[base : base + n], w_buf[...], preferred_element_type=jnp.float32)
        y = y.astype(jnp.bfloat16)
        for h in range(2):
            for part in range(3):
                left = h * 384 + part * 128
                value = y[:, left : left + 128]
                if part < 2:
                    value = normed(value, (gain_q, gain_k)[part][...])
                tall = value.astype(jnp.float32).reshape(n // 24, 3, 8, 128)
                for i in members:
                    line, lines = (starts[i] - base) // 24, rows[i] // 24
                    for tc in range(3):
                        stage[i, h, tc, 0 : lines * 8, part * 128 : part * 128 + 128] = (
                            tall[line : line + lines, tc]
                            .reshape(lines * 8, 128)
                            .astype(jnp.bfloat16)
                        )
        for i in members:
            blk, off = places[i]
            tall_rows = rows[i] // 3
            for h in range(2):
                copy = pltpu.make_async_copy(
                    stage.at[i, h, :, 0:tall_rows],
                    outs[h].at[:, blk, off : off + tall_rows],
                    out_sem.at[i, h],
                )
                copy.start()
                out_copies.append(copy)
    for copy in out_copies:
        copy.wait()


def project(xs, places, own_w, low_w, high_w, gain_q, gain_k):
    rows = [x.shape[0] for x in xs]
    count = len(xs)
    any_spec = pl.BlockSpec(memory_space=pl.ANY)
    vmem_spec = pl.BlockSpec(memory_space=pltpu.VMEM)

    def body(*refs):
        project_body(rows, places, *refs)

    return pl.pallas_call(
        body,
        out_shape=[jax.ShapeDtypeStruct((3, 4, 64, 384), jnp.bfloat16)] * 2,
        in_specs=[any_spec] * (count + 3) + [vmem_spec] * 2,
        out_specs=[any_spec] * 2,
        scratch_shapes=[
            pltpu.VMEM((sum(rows), D), jnp.bfloat16),
            pltpu.VMEM((D, 768), jnp.bfloat16),
            pltpu.VMEM((count, 2, 3, 64, 384), jnp.bfloat16),
            pltpu.SemaphoreType.DMA((count,)),
            pltpu.SemaphoreType.DMA((3,)),
            pltpu.SemaphoreType.DMA((count, 2)),
        ],
        compiler_params=pltpu.CompilerParams(vmem_limit_bytes=VMEM),
        cost_estimate=pl.CostEstimate(
            flops=2 * sum(rows) * D * 768,
            bytes_accessed=sum(rows) * D * 2 + D * 768 * 2,
            transcendentals=0,
        ),
        name="project",
    )(*xs, own_w, low_w, high_w, gain_q, gain_k)


def attend_body(
    near, far, s_near, s_far, x_near, x_far, picks_hbm, perm, out,
    q_buf, kv, v_t, even, odd, picks, sem,
):
    copies = []

    def fetch(src, dst):
        copy = pltpu.make_async_copy(src, dst, sem.at[len(copies)])
        copy.start()
        copies.append(copy)

    fetch(picks_hbm, picks)
    for h in range(2):
        for chunk, blocks, row, off in (
            (near, (0, 3), 0, 0), (far, (0, 1), 0, 3), (near, (3, 4), 1, 0), (far, (1, 4), 1, 1),
        ):
            tiles = pl.ds(h * 6 + row * 3, 3)
            there = pl.ds(off, blocks[1] - blocks[0])
            src = chunk[h].at[:, blocks[0] : blocks[1]]
            fetch(src.at[:, :, :, 0:HD], q_buf.at[tiles, there])
            fetch(src.at[:, :, :, HD : 3 * HD], kv.at[0, tiles, there])
    for g, (a, b) in ((1, (s_near, s_far)), (2, (x_near, x_far))):
        for h in range(2):
            for chunk, blocks, row, off in (
                (a, (0, 3), 0, 0), (b, (0, 1), 0, 3), (a, (3, 4), 1, 0), (b, (1, 4), 1, 1),
            ):
                fetch(
                    chunk.at[h, :, blocks[0] : blocks[1]],
                    kv.at[g, pl.ds(h * 6 + row * 3, 3), pl.ds(off, blocks[1] - blocks[0])],
                )
    for copy in copies:
        copy.wait()
    for g in range(3):

        @pl.loop(0, NT)
        def _(t):
            v_t[g, t] = kv[g, t, :, :, HD : 2 * HD].reshape(TILE, HD).T

    x_at, z = lax.axis_index("x"), lax.axis_index("z")
    rel_half, rel_core, core = lax.axis_index("yl"), lax.axis_index("yh"), lax.axis_index("c")
    rel_row, rel_z = z // 2, z % 2
    valid = jnp.where(core == 0, x_at, 3 - x_at)
    scale = HD**-0.5 * 1.4426950408889634
    shift = jnp.where(valid > 0, 0.0, 1e30).astype(jnp.float32)
    chunks = 3 * WIN

    def place(t):
        half = t // 6
        row = (t // 3) % 2
        return (half ^ rel_half) * 6 + (row ^ rel_row) * 3 + t % 3

    def places(t):
        return [place(picks[t, j]) for j in range(WIN)]

    def score(q, where, buf, n, tops):
        g, j = divmod(n, WIN)
        s = lax.dot_general(
            kv[g, where[j], :, :, 0:HD].reshape(TILE, HD),
            q,
            (((1,), (1,)), ((), ())),
            preferred_element_type=jnp.float32,
        )
        buf[n] = s
        high = jnp.max(s.reshape(TILE // 8, 8, TILE), axis=0)
        i = 1 if g == 2 else 0
        tops[i] = high if tops[i] is None else jnp.maximum(tops[i], high)

    def step(t, cur, nxt, tops):
        where = places(t)
        later = jnp.minimum(t + 1, NT - 1)
        where_next = places(later)
        q_next = q_buf[place(later)].reshape(TILE, HD)
        m = jnp.max(jnp.maximum(tops[0], tops[1] - shift), axis=0, keepdims=True) * scale
        m_far = m + shift
        tops_next = [None, None]
        total = jnp.zeros((8, TILE), jnp.float32)
        acc = jnp.zeros((HD, TILE), jnp.float32)
        for n in range(chunks):
            g, j = divmod(n, WIN)
            score(q_next, where_next, nxt, n, tops_next)
            p = jnp.exp2(cur[n] * scale - (m_far if g == 2 else m))
            total = total + jnp.sum(p.reshape(TILE // 8, 8, TILE), axis=0)
            acc = acc + jnp.dot(
                v_t[g, where[j]], p.astype(jnp.bfloat16), preferred_element_type=jnp.float32
            )
        attn = (acc / jnp.sum(total, axis=0, keepdims=True)).astype(jnp.bfloat16)
        raster = perm[pl.ds(t, 1), :]
        frame = (
            (raster >= 768).astype(jnp.int32)
            + (raster >= 1536).astype(jnp.int32)
            + (raster >= 2304).astype(jnp.int32)
        )
        rest = raster - 768 * frame
        line = (rest * 2731) >> 16
        column = (rest - 24 * line) & 7
        rank = (((line >> 2) & 1) ^ rel_z) * 2 + (((line >> 1) & 1) ^ rel_core)
        second = jnp.where(rank == 2, 0, jnp.where(rank == 3, 3, rank + 1))
        block = jnp.where((((t // 3) % 2) ^ rel_row) == 1, second, rank)
        inner = block * 64 + frame * 16 + (line & 1) * 8 + column
        pick = (lax.broadcasted_iota(jnp.int32, (TILE, TILE), 0) == inner).astype(jnp.float32)
        ordered = jnp.dot(
            attn, pick.astype(jnp.bfloat16), preferred_element_type=jnp.float32
        ).T.astype(jnp.bfloat16)
        for i in range(4):
            piece = 4 * t + i
            owner = piece // 3
            out[(owner % 2) ^ core, owner // 2, piece % 3] = ordered[i * 64 : i * 64 + 64]
        return tuple(tops_next)

    tops = [None, None]
    first = places(0)
    for n in range(chunks):
        score(q_buf[place(0)].reshape(TILE, HD), first, even, n, tops)

    def two(i, tops):
        tops = step(2 * i, even, odd, tops)
        return step(2 * i + 1, odd, even, tops)

    lax.fori_loop(0, NT // 2, two, tuple(tops))


def attend(near, far, s_near, s_far, x_near, x_far, picks, perm):
    any_spec = pl.BlockSpec(memory_space=pl.ANY)
    vmem_spec = pl.BlockSpec(memory_space=pltpu.VMEM)
    keys = 3 * WIN * TILE

    def body(n0, n1, f0, f1, *refs):
        attend_body((n0, n1), (f0, f1), *refs)

    return pl.pallas_call(
        body,
        out_shape=jax.ShapeDtypeStruct((2, 8, 3, 64, HD), jnp.bfloat16),
        in_specs=[any_spec] * 9 + [vmem_spec],
        out_specs=vmem_spec,
        scratch_shapes=[
            pltpu.VMEM((NT, 4, 64, HD), jnp.bfloat16),
            pltpu.VMEM((3, NT, 4, 64, 2 * HD), jnp.bfloat16),
            pltpu.VMEM((3, NT, HD, TILE), jnp.bfloat16),
            pltpu.VMEM((3 * WIN, TILE, TILE), jnp.float32),
            pltpu.VMEM((3 * WIN, TILE, TILE), jnp.float32),
            pltpu.SMEM((NT, WIN), jnp.int32),
            pltpu.SemaphoreType.DMA((40,)),
        ],
        compiler_params=pltpu.CompilerParams(vmem_limit_bytes=VMEM),
        cost_estimate=pl.CostEstimate(
            flops=4 * NT * TILE * keys * HD,
            bytes_accessed=6_000_000,
            transcendentals=NT * TILE * keys,
        ),
        name="attend",
    )(*near, *far, s_near, s_far, x_near, x_far, picks, perm)


def mix_body(attn, *refs):
    out = refs[8]
    core, half, z = lax.axis_index("c"), lax.axis_index("yl"), lax.axis_index("z")
    total = None
    for i in range(8):
        side, pair = i // 4, i % 4
        kind = core ^ side
        heads = [
            attn[kind, (half ^ (pair // 2)) * 4 + (z ^ k)] for k in ((0, 1), (3, 2))[pair % 2]
        ]
        flat = jnp.concatenate(heads, axis=-1)
        part = jnp.dot(flat, refs[i][...], preferred_element_type=jnp.float32)
        total = part if total is None else total + part
    out[...] = total.astype(jnp.bfloat16)


def mix(attn, w_here, w_there):
    step = 512
    return pl.pallas_call(
        mix_body,
        out_shape=jax.ShapeDtypeStruct((192, D), jnp.bfloat16),
        grid=(D // step,),
        in_specs=[pl.BlockSpec((2, 8, 192, HD), lambda i: (0, 0, 0, 0))]
        + [pl.BlockSpec((2 * HD, step), lambda i: (0, i))] * 8,
        out_specs=pl.BlockSpec((192, step), lambda i: (0, i)),
        compiler_params=pltpu.CompilerParams(vmem_limit_bytes=VMEM),
        cost_estimate=pl.CostEstimate(
            flops=2 * 192 * 2048 * D, bytes_accessed=14_000_000, transcendentals=0
        ),
        name="mix",
    )(attn.reshape(2, 8, 192, HD), *w_here, *w_there)


def per_device(video, w_qkv, w_out, q_gain, k_gain, tile_perm, window):
    c = lax.axis_index("c")
    own = video.reshape(192, D)
    own_w = w_qkv.reshape(D, 384)
    gain_q = q_gain.reshape(1, HD)
    gain_k = k_gain.reshape(1, HD)

    near = move(own, across(1))
    rear = move(own, across(3))
    own_other = move(own, swap_core)
    low_w = move(own_w[: D // 2], up)
    high_w = move(own_w[D // 2 :], down)
    near, rear, own_other, low_w, high_w, tile_perm, w_out = lax.optimization_barrier(
        (near, rear, own_other, low_w, high_w, tile_perm, w_out)
    )

    far_a = move(rear[:96], across(1))
    far_b = move(near[96:], across(3))
    near_other = move(near, swap_core)
    rear_other = move(rear, swap_core)
    raster = move(tile_perm.reshape(NT, TILE), regroup(0))
    close = project(
        [own, own_other, near, rear],
        [(0, 0), (1, 0), (2, 0), (3, 0)],
        own_w, low_w, high_w, gain_q, gain_k,
    )

    near0 = move(close[0], regroup(0))
    near1 = move(close[1], regroup(1))
    far_a, far_b = after(far_a, close[0]), after(far_b, close[0])
    far_a_other = move(far_a, swap_core)
    far_b_other = move(far_b, swap_core)
    w_own = after(w_out, far_a_other, far_b_other)
    w_near = move(w_own, across(1))
    w_rear = move(w_own, across(3))
    w_far = move(w_own, across(2))
    distant = project(
        [near_other, rear_other, far_a, far_b, far_a_other, far_b_other],
        [(0, 0), (3, 0), (1, 0), (1, 32), (2, 0), (2, 32)],
        own_w, low_w, high_w, gain_q, gain_k,
    )
    near0, near1 = after(near0, distant[0]), after(near1, distant[0])
    near_kv = jnp.stack([near0[..., HD:], near1[..., HD:]])
    s_near = move(near_kv, swap_core)
    x_near = move(near_kv, beside)
    far0 = move(distant[0], regroup(0))
    far1 = move(distant[1], regroup(1))
    far_kv = jnp.stack([far0[..., HD:], far1[..., HD:]])
    s_far = move(far_kv, swap_core)
    x_far = move(far_kv, beside)
    w_near, w_rear = after(w_near, far0, far1), after(w_rear, far0, far1)
    w_one = jnp.concatenate([w_own, w_near]).reshape(2 * HD, D)
    w_two = jnp.concatenate([w_rear, w_far]).reshape(2 * HD, D)
    w_three = move(w_one, up)
    w_four = move(w_two, down)
    w_here = [w_one, w_two, w_three, w_four]
    w_there = [move(w_one, swap_core), move(w_two, swap_core)]
    attn = attend((near0, near1), (far0, far1), s_near, s_far, x_near, x_far, window, raster)
    other = move(attn[1], swap_core)
    both = jnp.where(c == 0, jnp.stack([attn[0], other]), jnp.stack([other, attn[0]]))
    spread = lax.all_to_all(
        both.reshape(16, 192, HD), ("yh", "yl", "z"), 0, 0, tiled=True
    )
    w_there += [move(after(w_three, attn), swap_core), move(after(w_four, attn), swap_core)]
    return mix(spread, w_here, w_there)[None]


def solution(mesh):
    fine = Mesh(mesh.devices.reshape(SIZES), AXES)
    tm = ("x", "yh")
    space = ("yl", "z", "c")
    in_specs = (
        P(tm, space, None, None),
        P(None, space, None),
        P(space, None, None),
        P(),
        P(),
        P(tm, None),
        P(),
    )
    return jax.shard_map(
        per_device, mesh=fine, in_specs=in_specs, out_specs=P(tm, space, None), check_vma=False
    )
```

```python
import jax
import jax.numpy as jnp
from jax import lax
from jax.experimental import pallas as pl
from jax.experimental.pallas import tpu as pltpu
from jax.sharding import Mesh
from jax.sharding import PartitionSpec as P

D = 3072
HD = 128
NT = 12
TILE = 256
WIN = 6
AXES = ("x", "yh", "yl", "z", "c")
SIZES = (4, 2, 2, 4, 2)
VMEM = 60 * 1024 * 1024
MIXERS = [
    [((x * 4 + (yh ^ c) * 2 + yl) * 4 + z) * 2 + c for yh in range(2) for yl in range(2) for z in range(4)]
    for x in range(4)
    for c in range(2)
]


def move(value, target):
    pairs = []
    for x in range(4):
        for y in range(4):
            for z in range(4):
                for c in range(2):
                    goal = target(x, y, z, c)
                    if goal is None:
                        continue
                    a, b, d, e = goal
                    pairs.append(
                        (((x * 4 + y) * 4 + z) * 2 + c, ((a * 4 + b % 4) * 4 + d) * 2 + e)
                    )
    return lax.ppermute(value, AXES, pairs)


def after(value, *others):
    return lax.optimization_barrier((value,) + others)[0]


def across(k):
    return lambda x, y, z, c: (x, y, z ^ k, c)


def swap_core(x, y, z, c):
    return (x, y, z, 1 - c)


def up(x, y, z, c):
    return (x, y + 1, z, c)


def down(x, y, z, c):
    return (x, y - 1, z, c)


def regroup(k):
    return lambda x, y, z, c: (x, 2 * c + ((y & 1) ^ k), z, y >> 1)


def beside(x, y, z, c):
    if c == 1:
        return (x + 1, y, z, 0) if x < 3 else None
    return (x - 1, y, z, 1) if x > 0 else None


def normed(part, gain):
    wide = part.astype(jnp.float32)
    mean = jnp.mean(wide * wide, axis=-1, keepdims=True)
    return (wide * lax.rsqrt(mean + 1e-06) * gain).astype(jnp.bfloat16)


def project_body(rows, places, *refs):
    count = len(rows)
    xs = refs[:count]
    own_w, low_w, high_w, gain_q, gain_k, out0, out1 = refs[count : count + 7]
    outs = (out0, out1)
    x_buf, w_buf, stage, x_sem, w_sem, out_sem = refs[count + 7 :]
    half = D // 2
    starts = [sum(rows[:i]) for i in range(count)]
    w_copies = [
        pltpu.make_async_copy(own_w, w_buf.at[:, 0:384], w_sem.at[0]),
        pltpu.make_async_copy(low_w, w_buf.at[0:half, 384:768], w_sem.at[1]),
        pltpu.make_async_copy(high_w, w_buf.at[half:D, 384:768], w_sem.at[2]),
    ]
    for copy in w_copies:
        copy.start()
    x_copies = []
    for i in range(count):
        copy = pltpu.make_async_copy(
            xs[i], x_buf.at[starts[i] : starts[i] + rows[i]], x_sem.at[i]
        )
        copy.start()
        x_copies.append(copy)
    for copy in w_copies:
        copy.wait()
    out_copies = []
    at = 0
    while at < count:
        members = [at]
        while sum(rows[i] for i in members) < 384:
            members.append(members[-1] + 1)
        at = members[-1] + 1
        for i in members:
            x_copies[i].wait()
        base, n = starts[members[0]], 384
        y = jnp.dot(x_buf[base : base + n], w_buf[...], preferred_element_type=jnp.float32)
        y = y.astype(jnp.bfloat16)
        for h in range(2):
            for part in range(3):
                left = h * 384 + part * 128
                value = y[:, left : left + 128]
                if part < 2:
                    value = normed(value, (gain_q, gain_k)[part][...])
                tall = value.astype(jnp.float32).reshape(n // 24, 3, 8, 128)
                for i in members:
                    line, lines = (starts[i] - base) // 24, rows[i] // 24
                    for tc in range(3):
                        stage[i, h, tc, 0 : lines * 8, part * 128 : part * 128 + 128] = (
                            tall[line : line + lines, tc]
                            .reshape(lines * 8, 128)
                            .astype(jnp.bfloat16)
                        )
        for i in members:
            blk, off = places[i]
            tall_rows = rows[i] // 3
            for h in range(2):
                copy = pltpu.make_async_copy(
                    stage.at[i, h, :, 0:tall_rows],
                    outs[h].at[:, blk, off : off + tall_rows],
                    out_sem.at[i, h],
                )
                copy.start()
                out_copies.append(copy)
    for copy in out_copies:
        copy.wait()


def project(xs, places, own_w, low_w, high_w, gain_q, gain_k):
    rows = [x.shape[0] for x in xs]
    count = len(xs)
    any_spec = pl.BlockSpec(memory_space=pl.ANY)
    vmem_spec = pl.BlockSpec(memory_space=pltpu.VMEM)

    def body(*refs):
        project_body(rows, places, *refs)

    return pl.pallas_call(
        body,
        out_shape=[jax.ShapeDtypeStruct((3, 4, 64, 384), jnp.bfloat16)] * 2,
        in_specs=[any_spec] * (count + 3) + [vmem_spec] * 2,
        out_specs=[any_spec] * 2,
        scratch_shapes=[
            pltpu.VMEM((sum(rows), D), jnp.bfloat16),
            pltpu.VMEM((D, 768), jnp.bfloat16),
            pltpu.VMEM((count, 2, 3, 64, 384), jnp.bfloat16),
            pltpu.SemaphoreType.DMA((count,)),
            pltpu.SemaphoreType.DMA((3,)),
            pltpu.SemaphoreType.DMA((count, 2)),
        ],
        compiler_params=pltpu.CompilerParams(vmem_limit_bytes=VMEM),
        cost_estimate=pl.CostEstimate(
            flops=2 * sum(rows) * D * 768,
            bytes_accessed=sum(rows) * D * 2 + D * 768 * 2,
            transcendentals=0,
        ),
        name="project",
    )(*xs, own_w, low_w, high_w, gain_q, gain_k)


def attend_body(
    near, far, s_near, s_far, x_near, x_far, picks_hbm, perm, keep, send,
    q_buf, kv, v_t, even, odd, picks, sem,
):
    copies = []

    def fetch(src, dst):
        copy = pltpu.make_async_copy(src, dst, sem.at[len(copies)])
        copy.start()
        copies.append(copy)

    fetch(picks_hbm, picks)
    for h in range(2):
        for chunk, blocks, row, off in (
            (near, (0, 3), 0, 0), (far, (0, 1), 0, 3), (near, (3, 4), 1, 0), (far, (1, 4), 1, 1),
        ):
            tiles = pl.ds(h * 6 + row * 3, 3)
            there = pl.ds(off, blocks[1] - blocks[0])
            src = chunk[h].at[:, blocks[0] : blocks[1]]
            fetch(src.at[:, :, :, 0:HD], q_buf.at[tiles, there])
            fetch(src.at[:, :, :, HD : 3 * HD], kv.at[0, tiles, there])
    for g, (a, b) in ((1, (s_near, s_far)), (2, (x_near, x_far))):
        for h in range(2):
            for chunk, blocks, row, off in (
                (a, (0, 3), 0, 0), (b, (0, 1), 0, 3), (a, (3, 4), 1, 0), (b, (1, 4), 1, 1),
            ):
                fetch(
                    chunk.at[h, :, blocks[0] : blocks[1]],
                    kv.at[g, pl.ds(h * 6 + row * 3, 3), pl.ds(off, blocks[1] - blocks[0])],
                )
    for g, upto in ((0, 17), (1, 25), (2, 33)):
        for copy in copies[(0, 17, 25)[g] : upto]:
            copy.wait()

        @pl.loop(0, NT)
        def _(t):
            v_t[g, t] = kv[g, t, :, :, HD : 2 * HD].reshape(TILE, HD).T

    x_at, z = lax.axis_index("x"), lax.axis_index("z")
    rel_half, rel_core, core = lax.axis_index("yl"), lax.axis_index("yh"), lax.axis_index("c")
    rel_row, rel_z = z // 2, z % 2
    valid = jnp.where(core == 0, x_at, 3 - x_at)
    scale = HD**-0.5 * 1.4426950408889634
    shift = jnp.where(valid > 0, 0.0, 1e30).astype(jnp.float32)
    chunks = 3 * WIN

    def place(t):
        half = t // 6
        row = (t // 3) % 2
        return (half ^ rel_half) * 6 + (row ^ rel_row) * 3 + t % 3

    def places(t):
        return [place(picks[t, j]) for j in range(WIN)]

    def score(q, where, buf, n, tops):
        g, j = divmod(n, WIN)
        s = lax.dot_general(
            kv[g, where[j], :, :, 0:HD].reshape(TILE, HD),
            q,
            (((1,), (1,)), ((), ())),
            preferred_element_type=jnp.float32,
        )
        buf[n] = s
        high = jnp.max(s.reshape(TILE // 8, 8, TILE), axis=0)
        i = 1 if g == 2 else 0
        tops[i] = high if tops[i] is None else jnp.maximum(tops[i], high)

    def step(t, cur, nxt, tops):
        where = places(t)
        later = jnp.minimum(t + 1, NT - 1)
        where_next = places(later)
        q_next = q_buf[place(later)].reshape(TILE, HD)
        m = jnp.max(jnp.maximum(tops[0], tops[1] - shift), axis=0, keepdims=True) * scale
        m_far = m + shift
        tops_next = [None, None]
        total = jnp.zeros((8, TILE), jnp.float32)
        acc = jnp.zeros((HD, TILE), jnp.float32)
        for n in range(chunks):
            g, j = divmod(n, WIN)
            score(q_next, where_next, nxt, n, tops_next)
            p = jnp.exp2(cur[n] * scale - (m_far if g == 2 else m))
            total = total + jnp.sum(p.reshape(TILE // 8, 8, TILE), axis=0)
            acc = acc + jnp.dot(
                v_t[g, where[j]], p.astype(jnp.bfloat16), preferred_element_type=jnp.float32
            )
        attn = (acc / jnp.sum(total, axis=0, keepdims=True)).astype(jnp.bfloat16)
        raster = perm[:, pl.ds(pl.multiple_of(t * TILE, TILE), TILE)]
        frame = (
            (raster >= 768).astype(jnp.int32)
            + (raster >= 1536).astype(jnp.int32)
            + (raster >= 2304).astype(jnp.int32)
        )
        rest = raster - 768 * frame
        line = (rest * 2731) >> 16
        column = (rest - 24 * line) & 7
        rank = (((line >> 2) & 1) ^ rel_z) * 2 + (((line >> 1) & 1) ^ rel_core)
        second = jnp.where(rank == 2, 0, jnp.where(rank == 3, 3, rank + 1))
        block = jnp.where((((t // 3) % 2) ^ rel_row) == 1, second, rank)
        inner = block * 64 + frame * 16 + (line & 1) * 8 + column
        pick = (lax.broadcasted_iota(jnp.int32, (TILE, TILE), 0) == inner).astype(jnp.float32)
        ordered = jnp.dot(
            attn, pick.astype(jnp.bfloat16), preferred_element_type=jnp.float32
        ).T.astype(jnp.bfloat16)
        for i in range(4):
            piece = 4 * t + i
            owner = piece // 3
            rows = ordered[i * 64 : i * 64 + 64]

            @pl.when((owner % 2) == core)
            def _():
                keep[owner // 2, piece % 3] = rows

            @pl.when((owner % 2) != core)
            def _():
                send[owner // 2, piece % 3] = rows

        return tuple(tops_next)

    tops = [None, None]
    first = places(0)
    for n in range(chunks):
        score(q_buf[place(0)].reshape(TILE, HD), first, even, n, tops)

    def two(i, tops):
        tops = step(2 * i, even, odd, tops)
        return step(2 * i + 1, odd, even, tops)

    lax.fori_loop(0, NT // 2, two, tuple(tops))


def attend(near, far, s_near, s_far, x_near, x_far, picks, perm):
    any_spec = pl.BlockSpec(memory_space=pl.ANY)
    vmem_spec = pl.BlockSpec(memory_space=pltpu.VMEM)

    def body(n0, n1, f0, f1, *refs):
        attend_body((n0, n1), (f0, f1), *refs)

    return pl.pallas_call(
        body,
        out_shape=[jax.ShapeDtypeStruct((8, 3, 64, HD), jnp.bfloat16)] * 2,
        in_specs=[any_spec] * 9 + [vmem_spec],
        out_specs=[vmem_spec] * 2,
        scratch_shapes=[
            pltpu.VMEM((NT, 4, 64, HD), jnp.bfloat16),
            pltpu.VMEM((3, NT, 4, 64, 2 * HD), jnp.bfloat16),
            pltpu.VMEM((3, NT, HD, TILE), jnp.bfloat16),
            pltpu.VMEM((3 * WIN, TILE, TILE), jnp.float32),
            pltpu.VMEM((3 * WIN, TILE, TILE), jnp.float32),
            pltpu.SMEM((NT, WIN), jnp.int32),
            pltpu.SemaphoreType.DMA((40,)),
        ],
        compiler_params=pltpu.CompilerParams(vmem_limit_bytes=VMEM),
        cost_estimate=pl.CostEstimate(
            flops=32_000_000_000, bytes_accessed=6_000_000, transcendentals=0
        ),
        name="attend",
    )(*near, *far, s_near, s_far, x_near, x_far, picks, perm)


def mix_body(attn, *refs):
    out = refs[8]
    half, z = lax.axis_index("yl"), lax.axis_index("z")
    total = None
    for i in range(8):
        side, pair = i // 4, i % 4
        heads = [
            attn[side, (half ^ (pair // 2)) * 4 + (z ^ k)] for k in ((0, 1), (3, 2))[pair % 2]
        ]
        flat = jnp.concatenate(heads, axis=-1)
        part = jnp.dot(flat, refs[i][...], preferred_element_type=jnp.float32)
        total = part if total is None else total + part
    out[...] = total.astype(jnp.bfloat16)


def mix(attn, w_here, w_there):
    step = 512
    return pl.pallas_call(
        mix_body,
        out_shape=jax.ShapeDtypeStruct((192, D), jnp.bfloat16),
        grid=(D // step,),
        in_specs=[pl.BlockSpec((2, 8, 192, HD), lambda i: (0, 0, 0, 0))]
        + [pl.BlockSpec((2 * HD, step), lambda i: (0, i))] * 8,
        out_specs=pl.BlockSpec((192, step), lambda i: (0, i)),
        compiler_params=pltpu.CompilerParams(vmem_limit_bytes=VMEM),
        cost_estimate=pl.CostEstimate(
            flops=2 * 192 * 2048 * D, bytes_accessed=14_000_000, transcendentals=0
        ),
        name="mix",
    )(attn.reshape(2, 8, 192, HD), *w_here, *w_there)


def per_device(video, w_qkv, w_out, q_gain, k_gain, tile_perm, window):
    c = lax.axis_index("c")
    own = video.reshape(192, D)
    own_w = w_qkv.reshape(D, 384)
    gain_q = q_gain.reshape(1, HD)
    gain_k = k_gain.reshape(1, HD)

    near = move(own, across(1))
    rear = move(own, across(3))
    own_other = move(own, swap_core)
    low_w = move(own_w[: D // 2], up)
    high_w = move(own_w[D // 2 :], down)
    raster = move(tile_perm, regroup(0))
    near, rear, own_other, low_w, high_w, raster, w_out = lax.optimization_barrier(
        (near, rear, own_other, low_w, high_w, raster, w_out)
    )

    far_a = move(rear[:96], across(1))
    far_b = move(near[96:], across(3))
    near_other = move(near, swap_core)
    rear_other = move(rear, swap_core)
    close = project(
        [own, own_other, near, rear],
        [(0, 0), (1, 0), (2, 0), (3, 0)],
        own_w, low_w, high_w, gain_q, gain_k,
    )

    near0 = move(close[0], regroup(0))
    near1 = move(close[1], regroup(1))
    far_a, far_b = after(far_a, close[0]), after(far_b, close[0])
    far_a_other = move(far_a, swap_core)
    far_b_other = move(far_b, swap_core)
    w_own = after(w_out, far_a_other, far_b_other)
    w_near = move(w_own, across(1))
    w_rear = move(w_own, across(3))
    distant = project(
        [near_other, rear_other, far_a, far_b, far_a_other, far_b_other],
        [(0, 0), (3, 0), (1, 0), (1, 32), (2, 0), (2, 32)],
        own_w, low_w, high_w, gain_q, gain_k,
    )
    near0, near1 = after(near0, distant[0]), after(near1, distant[0])
    near_kv = jnp.stack([near0[..., HD:], near1[..., HD:]])
    s_near = move(near_kv, swap_core)
    x_near = move(near_kv, beside)
    w_far = move(after(w_own, distant[0]), across(2))
    far0 = move(after(distant[0], w_near, w_rear), regroup(0))
    far1 = move(after(distant[1], w_near, w_rear), regroup(1))
    far_kv = jnp.stack([far0[..., HD:], far1[..., HD:]])
    s_far = move(far_kv, swap_core)
    x_far = move(far_kv, beside)
    w_near, w_rear, w_far = (after(w, far0, far1) for w in (w_near, w_rear, w_far))
    w_one = jnp.concatenate([w_own, w_near]).reshape(2 * HD, D)
    w_two = jnp.concatenate([w_rear, w_far]).reshape(2 * HD, D)
    w_three = move(w_one, up)
    w_four = move(w_two, down)
    w_here = [w_one, w_two, w_three, w_four]
    w_there = [move(w_one, swap_core), move(w_two, swap_core)]
    keep, send = attend((near0, near1), (far0, far1), s_near, s_far, x_near, x_far, window, raster)
    received = move(send, swap_core)
    both = jnp.concatenate([keep, received])
    spread = lax.all_to_all(
        both.reshape(16, 192, HD), AXES, 0, 0, axis_index_groups=MIXERS, tiled=True
    )
    w_there += [move(after(w_three, received), swap_core), move(after(w_four, received), swap_core)]
    return mix(spread, w_here, w_there)[None]


def solution(mesh):
    fine = Mesh(mesh.devices.reshape(SIZES), AXES)
    tm = ("x", "yh")
    space = ("yl", "z", "c")
    in_specs = (
        P(tm, space, None, None),
        P(None, space, None),
        P(space, None, None),
        P(),
        P(),
        P(tm, None),
        P(),
    )
    return jax.shard_map(
        per_device, mesh=fine, in_specs=in_specs, out_specs=P(tm, space, None), check_vma=False
    )
```

```python
import jax
import jax.numpy as jnp
from jax import lax
from jax.experimental import pallas as pl
from jax.experimental.pallas import tpu as pltpu
from jax.sharding import Mesh
from jax.sharding import PartitionSpec as P

D = 3072
HD = 128
NT = 12
TILE = 256
WIN = 6
AXES = ("x", "yh", "yl", "z", "c")
SIZES = (4, 2, 2, 4, 2)
VMEM = 63 * 1024 * 1024
MIXERS = [
    [((x * 4 + (yh ^ c) * 2 + yl) * 4 + z) * 2 + c for yh in range(2) for yl in range(2) for z in range(4)]
    for x in range(4)
    for c in range(2)
]


def move(value, target):
    pairs = []
    for x in range(4):
        for y in range(4):
            for z in range(4):
                for c in range(2):
                    goal = target(x, y, z, c)
                    if goal is None:
                        continue
                    a, b, d, e = goal
                    pairs.append(
                        (((x * 4 + y) * 4 + z) * 2 + c, ((a * 4 + b % 4) * 4 + d) * 2 + e)
                    )
    return lax.ppermute(value, AXES, pairs)


def after(value, *others):
    return lax.optimization_barrier((value,) + others)[0]


def across(k):
    return lambda x, y, z, c: (x, y, z ^ k, c)


def swap_core(x, y, z, c):
    return (x, y, z, 1 - c)


def up(x, y, z, c):
    return (x, y + 1, z, c)


def down(x, y, z, c):
    return (x, y - 1, z, c)


def regroup(k):
    return lambda x, y, z, c: (x, 2 * c + ((y & 1) ^ k), z, y >> 1)


def beside(x, y, z, c):
    if c == 1:
        return (x + 1, y, z, 0) if x < 3 else None
    return (x - 1, y, z, 1) if x > 0 else None


def normed(part, gain):
    wide = part.astype(jnp.float32)
    mean = jnp.mean(wide * wide, axis=-1, keepdims=True)
    return (wide * lax.rsqrt(mean + 1e-06) * gain).astype(jnp.bfloat16)


def project_body(rows, places, *refs):
    count = len(rows)
    xs = refs[:count]
    own_w, low_w, high_w, gain_q, gain_k, out0, out1 = refs[count : count + 7]
    outs = (out0, out1)
    x_buf, w_buf, stage, x_sem, w_sem, out_sem = refs[count + 7 :]
    half = D // 2
    starts = [sum(rows[:i]) for i in range(count)]
    w_copies = [
        pltpu.make_async_copy(own_w, w_buf.at[:, 0:384], w_sem.at[0]),
        pltpu.make_async_copy(low_w, w_buf.at[0:half, 384:768], w_sem.at[1]),
        pltpu.make_async_copy(high_w, w_buf.at[half:D, 384:768], w_sem.at[2]),
    ]
    for copy in w_copies:
        copy.start()
    x_copies = []
    for i in range(count):
        copy = pltpu.make_async_copy(
            xs[i], x_buf.at[starts[i] : starts[i] + rows[i]], x_sem.at[i]
        )
        copy.start()
        x_copies.append(copy)
    for copy in w_copies:
        copy.wait()
    out_copies = []
    at = 0
    while at < count:
        members = [at]
        while sum(rows[i] for i in members) < 384:
            members.append(members[-1] + 1)
        at = members[-1] + 1
        for i in members:
            x_copies[i].wait()
        base, n = starts[members[0]], 384
        y = jnp.dot(x_buf[base : base + n], w_buf[...], preferred_element_type=jnp.float32)
        y = y.astype(jnp.bfloat16)
        for h in range(2):
            for part in range(3):
                left = h * 384 + part * 128
                value = y[:, left : left + 128]
                if part < 2:
                    value = normed(value, (gain_q, gain_k)[part][...])
                tall = value.astype(jnp.float32).reshape(n // 24, 3, 8, 128)
                for i in members:
                    line, lines = (starts[i] - base) // 24, rows[i] // 24
                    for tc in range(3):
                        stage[i, h, tc, 0 : lines * 8, part * 128 : part * 128 + 128] = (
                            tall[line : line + lines, tc]
                            .reshape(lines * 8, 128)
                            .astype(jnp.bfloat16)
                        )
        for i in members:
            blk, off = places[i]
            tall_rows = rows[i] // 3
            for h in range(2):
                copy = pltpu.make_async_copy(
                    stage.at[i, h, :, 0:tall_rows],
                    outs[h].at[:, blk, off : off + tall_rows],
                    out_sem.at[i, h],
                )
                copy.start()
                out_copies.append(copy)
    for copy in out_copies:
        copy.wait()


def project(xs, places, own_w, low_w, high_w, gain_q, gain_k):
    rows = [x.shape[0] for x in xs]
    count = len(xs)
    any_spec = pl.BlockSpec(memory_space=pl.ANY)
    vmem_spec = pl.BlockSpec(memory_space=pltpu.VMEM)

    def body(*refs):
        project_body(rows, places, *refs)

    return pl.pallas_call(
        body,
        out_shape=[jax.ShapeDtypeStruct((3, 4, 64, 384), jnp.bfloat16)] * 2,
        in_specs=[any_spec] * (count + 3) + [vmem_spec] * 2,
        out_specs=[any_spec] * 2,
        scratch_shapes=[
            pltpu.VMEM((sum(rows), D), jnp.bfloat16),
            pltpu.VMEM((D, 768), jnp.bfloat16),
            pltpu.VMEM((count, 2, 3, 64, 384), jnp.bfloat16),
            pltpu.SemaphoreType.DMA((count,)),
            pltpu.SemaphoreType.DMA((3,)),
            pltpu.SemaphoreType.DMA((count, 2)),
        ],
        compiler_params=pltpu.CompilerParams(vmem_limit_bytes=VMEM),
        cost_estimate=pl.CostEstimate(
            flops=2 * sum(rows) * D * 768,
            bytes_accessed=sum(rows) * D * 2 + D * 768 * 2,
            transcendentals=0,
        ),
        name="project",
    )(*xs, own_w, low_w, high_w, gain_q, gain_k)


def attend_body(
    near, far, s_near, s_far, x_near, x_far, picks_hbm, perm, keep, send,
    q_buf, kv, v_t, even, odd, picks, sem,
):
    copies = []

    def fetch(src, dst):
        copy = pltpu.make_async_copy(src, dst, sem.at[len(copies)])
        copy.start()
        copies.append(copy)

    fetch(picks_hbm, picks)
    for h in range(2):
        for chunk, blocks, row, off in (
            (near, (0, 3), 0, 0), (far, (0, 1), 0, 3), (near, (3, 4), 1, 0), (far, (1, 4), 1, 1),
        ):
            tiles = pl.ds(h * 6 + row * 3, 3)
            there = pl.ds(off, blocks[1] - blocks[0])
            src = chunk[h].at[:, blocks[0] : blocks[1]]
            fetch(src.at[:, :, :, 0:HD], q_buf.at[tiles, there])
            fetch(src.at[:, :, :, HD : 3 * HD], kv.at[0, tiles, there])
    for g, (a, b) in ((1, (s_near, s_far)), (2, (x_near, x_far))):
        for h in range(2):
            for chunk, blocks, row, off in (
                (a, (0, 3), 0, 0), (b, (0, 1), 0, 3), (a, (3, 4), 1, 0), (b, (1, 4), 1, 1),
            ):
                fetch(
                    chunk.at[h, :, blocks[0] : blocks[1]],
                    kv.at[g, pl.ds(h * 6 + row * 3, 3), pl.ds(off, blocks[1] - blocks[0])],
                )
    for g, upto in ((0, 17), (1, 25), (2, 33)):
        for copy in copies[(0, 17, 25)[g] : upto]:
            copy.wait()

        @pl.loop(0, NT)
        def _(t):
            v_t[g, t] = kv[g, t, :, :, HD : 2 * HD].reshape(TILE, HD).T

    x_at, z = lax.axis_index("x"), lax.axis_index("z")
    rel_half, rel_core, core = lax.axis_index("yl"), lax.axis_index("yh"), lax.axis_index("c")
    rel_row, rel_z = z // 2, z % 2
    valid = jnp.where(core == 0, x_at, 3 - x_at)
    scale = HD**-0.5 * 1.4426950408889634
    shift = jnp.where(valid > 0, 0.0, 1e30).astype(jnp.float32)
    chunks = 3 * WIN

    def place(t):
        half = t // 6
        row = (t // 3) % 2
        return (half ^ rel_half) * 6 + (row ^ rel_row) * 3 + t % 3

    def places(t):
        return [place(picks[t, j]) for j in range(WIN)]

    def score(q, where, buf, n, tops):
        g, j = divmod(n, WIN)
        s = lax.dot_general(
            kv[g, where[j], :, :, 0:HD].reshape(TILE, HD),
            q,
            (((1,), (1,)), ((), ())),
            preferred_element_type=jnp.float32,
        )
        buf[n] = s
        high = jnp.max(s.reshape(TILE // 8, 8, TILE), axis=0)
        i = 1 if g == 2 else 0
        tops[i] = high if tops[i] is None else jnp.maximum(tops[i], high)

    def step(t, cur, nxt, tops):
        where = places(t)
        later = jnp.minimum(t + 1, NT - 1)
        where_next = places(later)
        q_next = q_buf[place(later)].reshape(TILE, HD)
        m = jnp.max(jnp.maximum(tops[0], tops[1] - shift), axis=0, keepdims=True) * scale
        m_far = m + shift
        tops_next = [None, None]
        total = jnp.zeros((8, TILE), jnp.float32)
        acc = jnp.zeros((HD, TILE), jnp.float32)
        for n in range(chunks):
            g, j = divmod(n, WIN)
            score(q_next, where_next, nxt, n, tops_next)
            p = jnp.exp2(cur[n] * scale - (m_far if g == 2 else m))
            total = total + jnp.sum(p.reshape(TILE // 8, 8, TILE), axis=0)
            acc = acc + jnp.dot(
                v_t[g, where[j]], p.astype(jnp.bfloat16), preferred_element_type=jnp.float32
            )
        attn = (acc / jnp.sum(total, axis=0, keepdims=True)).astype(jnp.bfloat16)
        raster = perm[:, pl.ds(pl.multiple_of(t * TILE, TILE), TILE)]
        frame = (
            (raster >= 768).astype(jnp.int32)
            + (raster >= 1536).astype(jnp.int32)
            + (raster >= 2304).astype(jnp.int32)
        )
        rest = raster - 768 * frame
        line = (rest * 2731) >> 16
        column = (rest - 24 * line) & 7
        rank = (((line >> 2) & 1) ^ rel_z) * 2 + (((line >> 1) & 1) ^ rel_core)
        second = jnp.where(rank == 2, 0, jnp.where(rank == 3, 3, rank + 1))
        block = jnp.where((((t // 3) % 2) ^ rel_row) == 1, second, rank)
        inner = block * 64 + frame * 16 + (line & 1) * 8 + column
        pick = (lax.broadcasted_iota(jnp.int32, (TILE, TILE), 0) == inner).astype(jnp.float32)
        ordered = jnp.dot(
            attn, pick.astype(jnp.bfloat16), preferred_element_type=jnp.float32
        ).T.astype(jnp.bfloat16)
        for i in range(4):
            piece = 4 * t + i
            owner = piece // 3
            rows = ordered[i * 64 : i * 64 + 64]

            @pl.when((owner % 2) == core)
            def _():
                keep[owner // 2, piece % 3] = rows

            @pl.when((owner % 2) != core)
            def _():
                send[owner // 2, piece % 3] = rows

        return tuple(tops_next)

    tops = [None, None]
    first = places(0)
    for n in range(chunks):
        score(q_buf[place(0)].reshape(TILE, HD), first, even, n, tops)

    def two(i, tops):
        tops = step(2 * i, even, odd, tops)
        return step(2 * i + 1, odd, even, tops)

    lax.fori_loop(0, NT // 2, two, tuple(tops))


def attend(near, far, s_near, s_far, x_near, x_far, picks, perm):
    any_spec = pl.BlockSpec(memory_space=pl.ANY)
    vmem_spec = pl.BlockSpec(memory_space=pltpu.VMEM)

    def body(n0, n1, f0, f1, *refs):
        attend_body((n0, n1), (f0, f1), *refs)

    return pl.pallas_call(
        body,
        out_shape=[jax.ShapeDtypeStruct((8, 3, 64, HD), jnp.bfloat16)] * 2,
        in_specs=[any_spec] * 9 + [vmem_spec],
        out_specs=[vmem_spec] * 2,
        scratch_shapes=[
            pltpu.VMEM((NT, 4, 64, HD), jnp.bfloat16),
            pltpu.VMEM((3, NT, 4, 64, 2 * HD), jnp.bfloat16),
            pltpu.VMEM((3, NT, HD, TILE), jnp.bfloat16),
            pltpu.VMEM((3 * WIN, TILE, TILE), jnp.float32),
            pltpu.VMEM((3 * WIN, TILE, TILE), jnp.float32),
            pltpu.SMEM((NT, WIN), jnp.int32),
            pltpu.SemaphoreType.DMA((40,)),
        ],
        compiler_params=pltpu.CompilerParams(vmem_limit_bytes=VMEM),
        cost_estimate=pl.CostEstimate(
            flops=32_000_000_000, bytes_accessed=6_000_000, transcendentals=0
        ),
        name="attend",
    )(*near, *far, s_near, s_far, x_near, x_far, picks, perm)


def mix_body(attn, *refs):
    out = refs[8]
    half, z = lax.axis_index("yl"), lax.axis_index("z")
    total = None
    for i in range(8):
        side, pair = i // 4, i % 4
        heads = [
            attn[side, (half ^ (pair // 2)) * 4 + (z ^ k)] for k in ((0, 1), (3, 2))[pair % 2]
        ]
        flat = jnp.concatenate(heads, axis=-1)
        part = jnp.dot(flat, refs[i][...], preferred_element_type=jnp.float32)
        total = part if total is None else total + part
    out[...] = total.astype(jnp.bfloat16)


def mix(attn, w_here, w_there):
    step = 512
    return pl.pallas_call(
        mix_body,
        out_shape=jax.ShapeDtypeStruct((192, D), jnp.bfloat16),
        grid=(D // step,),
        in_specs=[pl.BlockSpec((2, 8, 192, HD), lambda i: (0, 0, 0, 0))]
        + [pl.BlockSpec((2 * HD, step), lambda i: (0, i))] * 8,
        out_specs=pl.BlockSpec((192, step), lambda i: (0, i)),
        compiler_params=pltpu.CompilerParams(vmem_limit_bytes=VMEM),
        cost_estimate=pl.CostEstimate(
            flops=2 * 192 * 2048 * D, bytes_accessed=14_000_000, transcendentals=0
        ),
        name="mix",
    )(attn.reshape(2, 8, 192, HD), *w_here, *w_there)


def per_device(video, w_qkv, w_out, q_gain, k_gain, tile_perm, window):
    c = lax.axis_index("c")
    own = video.reshape(192, D)
    own_w = w_qkv.reshape(D, 384)
    gain_q = q_gain.reshape(1, HD)
    gain_k = k_gain.reshape(1, HD)

    near = move(own, across(1))
    rear = move(own, across(3))
    own_other = move(own, swap_core)
    low_w = move(own_w[: D // 2], up)
    high_w = move(own_w[D // 2 :], down)
    raster = move(tile_perm, regroup(0))
    near, rear, own_other, low_w, high_w, raster, w_out = lax.optimization_barrier(
        (near, rear, own_other, low_w, high_w, raster, w_out)
    )

    far_a = move(rear[:96], across(1))
    far_b = move(near[96:], across(3))
    near_other = move(near, swap_core)
    rear_other = move(rear, swap_core)
    close = project(
        [own, own_other, near, rear],
        [(0, 0), (1, 0), (2, 0), (3, 0)],
        own_w, low_w, high_w, gain_q, gain_k,
    )

    near0 = move(close[0], regroup(0))
    near1 = move(close[1], regroup(1))
    far_a, far_b = after(far_a, close[0]), after(far_b, close[0])
    far_a_other = move(far_a, swap_core)
    far_b_other = move(far_b, swap_core)
    w_own = after(w_out, far_a_other, far_b_other)
    w_near = move(w_own, across(1))
    w_rear = move(w_own, across(3))
    distant = project(
        [near_other, rear_other, far_a, far_b, far_a_other, far_b_other],
        [(0, 0), (3, 0), (1, 0), (1, 32), (2, 0), (2, 32)],
        own_w, low_w, high_w, gain_q, gain_k,
    )
    near0, near1 = after(near0, distant[0]), after(near1, distant[0])
    near_kv = jnp.stack([near0[..., HD:], near1[..., HD:]])
    s_near = move(near_kv, swap_core)
    x_near = move(near_kv, beside)
    w_far = move(after(w_own, distant[0]), across(2))
    far0 = move(after(distant[0], w_near, w_rear), regroup(0))
    far1 = move(after(distant[1], w_near, w_rear), regroup(1))
    far_kv = jnp.stack([far0[..., HD:], far1[..., HD:]])
    s_far = move(far_kv, swap_core)
    x_far = move(far_kv, beside)
    w_near, w_rear, w_far = (after(w, far0, far1) for w in (w_near, w_rear, w_far))
    w_one = jnp.concatenate([w_own, w_near]).reshape(2 * HD, D)
    w_two = jnp.concatenate([w_rear, w_far]).reshape(2 * HD, D)
    w_three = move(w_one, up)
    w_four = move(w_two, down)
    w_here = [w_one, w_two, w_three, w_four]
    w_there = [move(w_one, swap_core), move(w_two, swap_core)]
    keep, send = attend((near0, near1), (far0, far1), s_near, s_far, x_near, x_far, window, raster)
    received = move(send, swap_core)
    both = jnp.concatenate([keep, received])
    spread = lax.all_to_all(
        both.reshape(16, 192, HD), AXES, 0, 0, axis_index_groups=MIXERS, tiled=True
    )
    w_there += [move(after(w_three, received), swap_core), move(after(w_four, received), swap_core)]
    return mix(spread, w_here, w_there)[None]


def solution(mesh):
    fine = Mesh(mesh.devices.reshape(SIZES), AXES)
    tm = ("x", "yh")
    space = ("yl", "z", "c")
    in_specs = (
        P(tm, space, None, None),
        P(None, space, None),
        P(space, None, None),
        P(),
        P(),
        P(tm, None),
        P(),
    )
    return jax.shard_map(
        per_device, mesh=fine, in_specs=in_specs, out_specs=P(tm, space, None), check_vma=False
    )
```

```python
import jax
import jax.numpy as jnp
from jax import lax
from jax.experimental import pallas as pl
from jax.experimental.pallas import tpu as pltpu
from jax.sharding import Mesh
from jax.sharding import PartitionSpec as P

D = 3072
HD = 128
NT = 12
TILE = 256
WIN = 6
AXES = ("x", "yh", "yl", "z", "c")
SIZES = (4, 2, 2, 4, 2)
VMEM = 40 * 1024 * 1024
MIXERS = [
    [((x * 4 + (yh ^ c) * 2 + yl) * 4 + z) * 2 + c for yh in range(2) for yl in range(2) for z in range(4)]
    for x in range(4)
    for c in range(2)
]


def move(value, target):
    pairs = []
    for x in range(4):
        for y in range(4):
            for z in range(4):
                for c in range(2):
                    goal = target(x, y, z, c)
                    if goal is None:
                        continue
                    a, b, d, e = goal
                    pairs.append(
                        (((x * 4 + y) * 4 + z) * 2 + c, ((a * 4 + b % 4) * 4 + d) * 2 + e)
                    )
    return lax.ppermute(value, AXES, pairs)


def after(value, *others):
    return lax.optimization_barrier((value,) + others)[0]


def across(k):
    return lambda x, y, z, c: (x, y, z ^ k, c)


def swap_core(x, y, z, c):
    return (x, y, z, 1 - c)


def up(x, y, z, c):
    return (x, y + 1, z, c)


def down(x, y, z, c):
    return (x, y - 1, z, c)


def regroup(k):
    return lambda x, y, z, c: (x, 2 * c + ((y & 1) ^ k), z, y >> 1)


def beside(x, y, z, c):
    if c == 1:
        return (x + 1, y, z, 0) if x < 3 else None
    return (x - 1, y, z, 1) if x > 0 else None


def normed(part, gain):
    wide = part.astype(jnp.float32)
    mean = jnp.mean(wide * wide, axis=-1, keepdims=True)
    return (wide * lax.rsqrt(mean + 1e-06) * gain).astype(jnp.bfloat16)


def project_body(rows, places, *refs):
    count = len(rows)
    xs = refs[:count]
    own_w, low_w, high_w, gain_q, gain_k, out0, out1 = refs[count : count + 7]
    outs = (out0, out1)
    x_buf, w_buf, stage, x_sem, w_sem, out_sem = refs[count + 7 :]
    half = D // 2
    starts = [sum(rows[:i]) for i in range(count)]
    w_copies = [
        pltpu.make_async_copy(own_w, w_buf.at[:, 0:384], w_sem.at[0]),
        pltpu.make_async_copy(low_w, w_buf.at[0:half, 384:768], w_sem.at[1]),
        pltpu.make_async_copy(high_w, w_buf.at[half:D, 384:768], w_sem.at[2]),
    ]
    for copy in w_copies:
        copy.start()
    x_copies = []
    for i in range(count):
        copy = pltpu.make_async_copy(
            xs[i], x_buf.at[starts[i] : starts[i] + rows[i]], x_sem.at[i]
        )
        copy.start()
        x_copies.append(copy)
    for copy in w_copies:
        copy.wait()
    out_copies = []
    at = 0
    while at < count:
        members = [at]
        while sum(rows[i] for i in members) < 384:
            members.append(members[-1] + 1)
        at = members[-1] + 1
        for i in members:
            x_copies[i].wait()
        base, n = starts[members[0]], 384
        y = jnp.dot(x_buf[base : base + n], w_buf[...], preferred_element_type=jnp.float32)
        y = y.astype(jnp.bfloat16)
        for h in range(2):
            for part in range(3):
                left = h * 384 + part * 128
                value = y[:, left : left + 128]
                if part < 2:
                    value = normed(value, (gain_q, gain_k)[part][...])
                tall = value.astype(jnp.float32).reshape(n // 24, 3, 8, 128)
                for i in members:
                    line, lines = (starts[i] - base) // 24, rows[i] // 24
                    for tc in range(3):
                        stage[i, h, tc, 0 : lines * 8, part * 128 : part * 128 + 128] = (
                            tall[line : line + lines, tc]
                            .reshape(lines * 8, 128)
                            .astype(jnp.bfloat16)
                        )
        for i in members:
            blk, off = places[i]
            tall_rows = rows[i] // 3
            for h in range(2):
                copy = pltpu.make_async_copy(
                    stage.at[i, h, :, 0:tall_rows],
                    outs[h].at[:, blk, off : off + tall_rows],
                    out_sem.at[i, h],
                )
                copy.start()
                out_copies.append(copy)
    for copy in out_copies:
        copy.wait()


def project(xs, places, own_w, low_w, high_w, gain_q, gain_k):
    rows = [x.shape[0] for x in xs]
    count = len(xs)
    any_spec = pl.BlockSpec(memory_space=pl.ANY)
    vmem_spec = pl.BlockSpec(memory_space=pltpu.VMEM)

    def body(*refs):
        project_body(rows, places, *refs)

    return pl.pallas_call(
        body,
        out_shape=[jax.ShapeDtypeStruct((3, 4, 64, 384), jnp.bfloat16)] * 2,
        in_specs=[any_spec] * (count + 3) + [vmem_spec] * 2,
        out_specs=[any_spec] * 2,
        scratch_shapes=[
            pltpu.VMEM((sum(rows), D), jnp.bfloat16),
            pltpu.VMEM((D, 768), jnp.bfloat16),
            pltpu.VMEM((count, 2, 3, 64, 384), jnp.bfloat16),
            pltpu.SemaphoreType.DMA((count,)),
            pltpu.SemaphoreType.DMA((3,)),
            pltpu.SemaphoreType.DMA((count, 2)),
        ],
        compiler_params=pltpu.CompilerParams(vmem_limit_bytes=VMEM),
        cost_estimate=pl.CostEstimate(
            flops=2 * sum(rows) * D * 768,
            bytes_accessed=sum(rows) * D * 2 + D * 768 * 2,
            transcendentals=0,
        ),
        name="project",
    )(*xs, own_w, low_w, high_w, gain_q, gain_k)


def attend_body(
    near, far, s_near, s_far, x_near, x_far, picks_hbm, perm, keep, send,
    q_buf, kv, v_t, even, odd, picks, sem,
):
    copies = []

    def fetch(src, dst):
        copy = pltpu.make_async_copy(src, dst, sem.at[len(copies)])
        copy.start()
        copies.append(copy)

    fetch(picks_hbm, picks)
    for h in range(2):
        for chunk, blocks, row, off in (
            (near, (0, 3), 0, 0), (far, (0, 1), 0, 3), (near, (3, 4), 1, 0), (far, (1, 4), 1, 1),
        ):
            tiles = pl.ds(h * 6 + row * 3, 3)
            there = pl.ds(off, blocks[1] - blocks[0])
            src = chunk[h].at[:, blocks[0] : blocks[1]]
            fetch(src.at[:, :, :, 0:HD], q_buf.at[tiles, there])
            fetch(src.at[:, :, :, HD : 3 * HD], kv.at[0, tiles, there])
    for g, (a, b) in ((1, (s_near, s_far)), (2, (x_near, x_far))):
        for h in range(2):
            for chunk, blocks, row, off in (
                (a, (0, 3), 0, 0), (b, (0, 1), 0, 3), (a, (3, 4), 1, 0), (b, (1, 4), 1, 1),
            ):
                fetch(
                    chunk.at[h, :, blocks[0] : blocks[1]],
                    kv.at[g, pl.ds(h * 6 + row * 3, 3), pl.ds(off, blocks[1] - blocks[0])],
                )
    for g, upto in ((0, 17), (1, 25), (2, 33)):
        for copy in copies[(0, 17, 25)[g] : upto]:
            copy.wait()

        @pl.loop(0, NT)
        def _(t):
            v_t[g, t] = kv[g, t, :, :, HD : 2 * HD].reshape(TILE, HD).T

    x_at, z = lax.axis_index("x"), lax.axis_index("z")
    rel_half, rel_core, core = lax.axis_index("yl"), lax.axis_index("yh"), lax.axis_index("c")
    rel_row, rel_z = z // 2, z % 2
    valid = jnp.where(core == 0, x_at, 3 - x_at)
    scale = HD**-0.5 * 1.4426950408889634
    shift = jnp.where(valid > 0, 0.0, 1e30).astype(jnp.float32)
    chunks = 3 * WIN

    def place(t):
        half = t // 6
        row = (t // 3) % 2
        return (half ^ rel_half) * 6 + (row ^ rel_row) * 3 + t % 3

    def places(t):
        return [place(picks[t, j]) for j in range(WIN)]

    def score(q, where, buf, n, tops):
        g, j = divmod(n, WIN)
        s = lax.dot_general(
            kv[g, where[j], :, :, 0:HD].reshape(TILE, HD),
            q,
            (((1,), (1,)), ((), ())),
            preferred_element_type=jnp.float32,
        )
        buf[n] = s
        high = jnp.max(s.reshape(TILE // 8, 8, TILE), axis=0)
        i = 1 if g == 2 else 0
        tops[i] = high if tops[i] is None else jnp.maximum(tops[i], high)

    def step(t, cur, nxt, tops):
        where = places(t)
        later = jnp.minimum(t + 1, NT - 1)
        where_next = places(later)
        q_next = q_buf[place(later)].reshape(TILE, HD)
        m = jnp.max(jnp.maximum(tops[0], tops[1] - shift), axis=0, keepdims=True) * scale
        m_far = m + shift
        tops_next = [None, None]
        total = jnp.zeros((8, TILE), jnp.float32)
        acc = jnp.zeros((HD, TILE), jnp.float32)
        for n in range(chunks):
            g, j = divmod(n, WIN)
            score(q_next, where_next, nxt, n, tops_next)
            p = jnp.exp2(cur[n] * scale - (m_far if g == 2 else m))
            total = total + jnp.sum(p.reshape(TILE // 8, 8, TILE), axis=0)
            acc = acc + jnp.dot(
                v_t[g, where[j]], p.astype(jnp.bfloat16), preferred_element_type=jnp.float32
            )
        attn = (acc / jnp.sum(total, axis=0, keepdims=True)).astype(jnp.bfloat16)
        raster = perm[:, pl.ds(pl.multiple_of(t * TILE, TILE), TILE)]
        frame = (
            (raster >= 768).astype(jnp.int32)
            + (raster >= 1536).astype(jnp.int32)
            + (raster >= 2304).astype(jnp.int32)
        )
        rest = raster - 768 * frame
        line = (rest * 2731) >> 16
        column = (rest - 24 * line) & 7
        rank = (((line >> 2) & 1) ^ rel_z) * 2 + (((line >> 1) & 1) ^ rel_core)
        second = jnp.where(rank == 2, 0, jnp.where(rank == 3, 3, rank + 1))
        block = jnp.where((((t // 3) % 2) ^ rel_row) == 1, second, rank)
        inner = block * 64 + frame * 16 + (line & 1) * 8 + column
        pick = (lax.broadcasted_iota(jnp.int32, (TILE, TILE), 0) == inner).astype(jnp.float32)
        ordered = jnp.dot(
            attn, pick.astype(jnp.bfloat16), preferred_element_type=jnp.float32
        ).T.astype(jnp.bfloat16)
        for i in range(4):
            piece = 4 * t + i
            owner = piece // 3
            rows = ordered[i * 64 : i * 64 + 64]

            @pl.when((owner % 2) == core)
            def _():
                keep[owner // 2, piece % 3] = rows

            @pl.when((owner % 2) != core)
            def _():
                send[owner // 2, piece % 3] = rows

        return tuple(tops_next)

    tops = [None, None]
    first = places(0)
    for n in range(chunks):
        score(q_buf[place(0)].reshape(TILE, HD), first, even, n, tops)

    def two(i, tops):
        tops = step(2 * i, even, odd, tops)
        return step(2 * i + 1, odd, even, tops)

    lax.fori_loop(0, NT // 2, two, tuple(tops))


def attend(near, far, s_near, s_far, x_near, x_far, picks, perm):
    any_spec = pl.BlockSpec(memory_space=pl.ANY)
    vmem_spec = pl.BlockSpec(memory_space=pltpu.VMEM)

    def body(n0, n1, f0, f1, *refs):
        attend_body((n0, n1), (f0, f1), *refs)

    return pl.pallas_call(
        body,
        out_shape=[jax.ShapeDtypeStruct((8, 3, 64, HD), jnp.bfloat16)] * 2,
        in_specs=[any_spec] * 9 + [vmem_spec],
        out_specs=[vmem_spec] * 2,
        scratch_shapes=[
            pltpu.VMEM((NT, 4, 64, HD), jnp.bfloat16),
            pltpu.VMEM((3, NT, 4, 64, 2 * HD), jnp.bfloat16),
            pltpu.VMEM((3, NT, HD, TILE), jnp.bfloat16),
            pltpu.VMEM((3 * WIN, TILE, TILE), jnp.float32),
            pltpu.VMEM((3 * WIN, TILE, TILE), jnp.float32),
            pltpu.SMEM((NT, WIN), jnp.int32),
            pltpu.SemaphoreType.DMA((40,)),
        ],
        compiler_params=pltpu.CompilerParams(vmem_limit_bytes=VMEM),
        cost_estimate=pl.CostEstimate(
            flops=32_000_000_000, bytes_accessed=6_000_000, transcendentals=0
        ),
        name="attend",
    )(*near, *far, s_near, s_far, x_near, x_far, picks, perm)


def mix_body(attn, *refs):
    out = refs[8]
    half, z = lax.axis_index("yl"), lax.axis_index("z")
    total = None
    for i in range(8):
        side, pair = i // 4, i % 4
        heads = [
            attn[side, (half ^ (pair // 2)) * 4 + (z ^ k)] for k in ((0, 1), (3, 2))[pair % 2]
        ]
        flat = jnp.concatenate(heads, axis=-1)
        part = jnp.dot(flat, refs[i][...], preferred_element_type=jnp.float32)
        total = part if total is None else total + part
    out[...] = total.astype(jnp.bfloat16)


def mix(attn, w_here, w_there):
    step = 512
    return pl.pallas_call(
        mix_body,
        out_shape=jax.ShapeDtypeStruct((192, D), jnp.bfloat16),
        grid=(D // step,),
        in_specs=[pl.BlockSpec((2, 8, 192, HD), lambda i: (0, 0, 0, 0))]
        + [pl.BlockSpec((2 * HD, step), lambda i: (0, i))] * 8,
        out_specs=pl.BlockSpec((192, step), lambda i: (0, i)),
        compiler_params=pltpu.CompilerParams(vmem_limit_bytes=VMEM),
        cost_estimate=pl.CostEstimate(
            flops=2 * 192 * 2048 * D, bytes_accessed=14_000_000, transcendentals=0
        ),
        name="mix",
    )(attn.reshape(2, 8, 192, HD), *w_here, *w_there)


def per_device(video, w_qkv, w_out, q_gain, k_gain, tile_perm, window):
    c = lax.axis_index("c")
    own = video.reshape(192, D)
    own_w = w_qkv.reshape(D, 384)
    gain_q = q_gain.reshape(1, HD)
    gain_k = k_gain.reshape(1, HD)

    near = move(own, across(1))
    rear = move(own, across(3))
    own_other = move(own, swap_core)
    low_w = move(own_w[: D // 2], up)
    high_w = move(own_w[D // 2 :], down)
    raster = move(tile_perm, regroup(0))
    near, rear, own_other, low_w, high_w, raster, w_out = lax.optimization_barrier(
        (near, rear, own_other, low_w, high_w, raster, w_out)
    )

    far_a = move(rear[:96], across(1))
    far_b = move(near[96:], across(3))
    near_other = move(near, swap_core)
    rear_other = move(rear, swap_core)
    close = project(
        [own, own_other, near, rear],
        [(0, 0), (1, 0), (2, 0), (3, 0)],
        own_w, low_w, high_w, gain_q, gain_k,
    )

    near0 = move(close[0], regroup(0))
    near1 = move(close[1], regroup(1))
    far_a, far_b = after(far_a, close[0]), after(far_b, close[0])
    far_a_other = move(far_a, swap_core)
    far_b_other = move(far_b, swap_core)
    w_own = after(w_out, far_a_other, far_b_other)
    w_near = move(w_own, across(1))
    w_rear = move(w_own, across(3))
    distant = project(
        [near_other, rear_other, far_a, far_b, far_a_other, far_b_other],
        [(0, 0), (3, 0), (1, 0), (1, 32), (2, 0), (2, 32)],
        own_w, low_w, high_w, gain_q, gain_k,
    )
    near0, near1 = after(near0, distant[0]), after(near1, distant[0])
    near_kv = jnp.stack([near0[..., HD:], near1[..., HD:]])
    s_near = move(near_kv, swap_core)
    x_near = move(near_kv, beside)
    w_far = move(after(w_own, distant[0]), across(2))
    far0 = move(after(distant[0], w_near, w_rear), regroup(0))
    far1 = move(after(distant[1], w_near, w_rear), regroup(1))
    far_kv = jnp.stack([far0[..., HD:], far1[..., HD:]])
    s_far = move(far_kv, swap_core)
    x_far = move(far_kv, beside)
    w_near, w_rear, w_far = (after(w, far0, far1) for w in (w_near, w_rear, w_far))
    w_one = jnp.concatenate([w_own, w_near]).reshape(2 * HD, D)
    w_two = jnp.concatenate([w_rear, w_far]).reshape(2 * HD, D)
    w_three = move(w_one, up)
    w_four = move(w_two, down)
    w_here = [w_one, w_two, w_three, w_four]
    w_there = [move(w_one, swap_core), move(w_two, swap_core)]
    keep, send = attend((near0, near1), (far0, far1), s_near, s_far, x_near, x_far, window, raster)
    received = move(send, swap_core)
    both = jnp.concatenate([keep, received])
    spread = lax.all_to_all(
        both.reshape(16, 192, HD), AXES, 0, 0, axis_index_groups=MIXERS, tiled=True
    )
    w_there += [move(after(w_three, received), swap_core), move(after(w_four, received), swap_core)]
    return mix(spread, w_here, w_there)[None]


def solution(mesh):
    fine = Mesh(mesh.devices.reshape(SIZES), AXES)
    tm = ("x", "yh")
    space = ("yl", "z", "c")
    in_specs = (
        P(tm, space, None, None),
        P(None, space, None),
        P(space, None, None),
        P(),
        P(),
        P(tm, None),
        P(),
    )
    return jax.shard_map(
        per_device, mesh=fine, in_specs=in_specs, out_specs=P(tm, space, None), check_vma=False
    )
```
